32 devices in a mesh: group: 4 (over x, core), dev: 8 (over z, y).
Axes of the slice: x: 2, y: 2, z: 4, core: 2. Of those that a mesh axis runs over, the one named last changes fastest.
Arguments:
- couplings: bfloat16 [32, 6, 4, 512, 512], P(('group', 'dev')), may hold values from -0.0625 to 0.0625
- history: bfloat16 [32, 16384, 256], P(None, ('group', 'dev')), may hold values from -6 to 6
- diag_inverse: bfloat16 [32, 512, 512], P(('group', 'dev')), may hold values from -0.25 to 0.25
- incident: bfloat16 [2, 16384, 256], P(None, ('group', 'dev')), may hold values from -6 to 6
- targets: int32 [32, 6], P(('group', 'dev')), may hold values from 0 to 10
- delays: int32 [32, 6], P(('group', 'dev')), may hold values from 1 to 29
- counts: int32 [32], P(('group', 'dev')), may hold values from 1 to 6, as said below
Outputs:
- currents: bfloat16 [2, 16384, 256], P(None, ('group', 'dev'))
The draws below stay inside these ranges and needn't reach their ends.
Inputs may be any that keep to these rules, and one draw needn't show every extreme that they name: `counts`: slots beyond a block's count carry matrices that are not couplings. Some block uses all 6 slots.
All inputs are finite; a program needn't handle non-finite values.
Results may differ from the reference program's by a relative error of at most 0.0048.
Values sent between devices are 32-bit elements; how exact they have to be, the bound alone decides.
No kernel may reach another device: no remote copies, remote signals or barrier semaphores. Data moves between devices by JAX's collectives and lax.ppermute only.
A program may use at most 128 MiB of HBM per device.

```python
import jax
import jax.numpy as jnp
from jax import lax

UNK = 512
EXC = 256
HIST = 32
BAND = 4
SLOTS = 6
STEPS = 2
BLOCKS = 32
UNKNOWNS = 16384
N_GROUP = 4
N_DEV = 8


def draw_counts(key, part):
    key_base, key_heavy, key_pick = jax.random.split(key, 3)
    light_load = jax.random.randint(key_base, (BLOCKS,), 1, SLOTS // 2 + 1)
    heavy_mask = jax.random.randint(key_heavy, (BLOCKS,), 0, 8) == 0
    chosen_block = jax.random.randint(key_pick, (), 0, BLOCKS)
    full_mask = heavy_mask | (jnp.arange(BLOCKS) == chosen_block)
    return jnp.where(full_mask, SLOTS, light_load).astype(jnp.int32)


def set_ends(entries, key, low, largest):
    extent = entries.shape
    spot = [jax.random.randint(jax.random.fold_in(key, axis), (), 0, extent[axis]) for axis in range(len(extent))]
    entries = entries.at[tuple(spot)].set(low)
    longest = extent.index(max(extent))
    spot[longest] = (spot[longest] + 1) % extent[longest]
    return entries.at[tuple(spot)].set(largest)


def block_scale(rng, dims, cuts, low, largest):
    level = 1.0
    for dim, blocks in cuts:
        steps = jax.random.uniform(jax.random.fold_in(jax.random.fold_in(rng, 6), dim), (blocks,), jnp.float32, low / len(cuts), largest / len(cuts))
        level = level * jnp.repeat(jnp.exp(steps), dims[dim] // blocks).reshape((-1,) + (1,) * (len(dims) - 1 - dim))
    return level


def normal_values(stream_key, extent, scale, bound, cuts=(), held_as=jnp.bfloat16):
    values = scale * jax.random.normal(stream_key, extent, jnp.float32)
    if cuts:
        values = values * block_scale(stream_key, extent, cuts, -0.22, 0.18)
    return jnp.clip(values, -bound, bound).astype(held_as)


def setup_inputs(seed: int = 0) -> dict:
    keys = jax.random.split(jax.random.key(seed), 8)
    return {
        "couplings": normal_values(keys[0], (BLOCKS, SLOTS, BAND, UNK, UNK), (4 * BAND * UNK) ** -0.5, 0.0625, ((0, 32),)),
        "history": normal_values(keys[1], (HIST, UNKNOWNS, EXC), 1.0, 6.0, ((1, 32),)),
        "diag_inverse": normal_values(keys[2], (BLOCKS, UNK, UNK), UNK ** -0.5, 0.25, ((0, 32),)),
        "incident": normal_values(keys[3], (STEPS, UNKNOWNS, EXC), 1.0, 6.0, ((1, 32),)),
        "targets": set_ends(jax.random.randint(keys[4], (BLOCKS, SLOTS), 0, 11), jax.random.fold_in(keys[4], 1), 0, 10).astype(jnp.int32),
        "delays": set_ends(jax.random.randint(keys[5], (BLOCKS, SLOTS), 1, HIST - BAND + 2), jax.random.fold_in(keys[5], 1), 1, (HIST - BAND + 2) - 1).astype(jnp.int32),
        "counts": draw_counts(jax.random.fold_in(keys[7], 71), 0),
    }


def code_offsets(target_code):
    if target_code < 5:
        return 0, target_code - 2
    if target_code < 8:
        return 1, target_code - 6
    return -1, target_code - 9


def reference(couplings, history, diag_inverse, incident, targets, delays, counts):
    recent = history
    outputs = []
    for moment in range(STEPS):
        def block_terms(block_id):
            matrices = couplings[block_id].astype(jnp.float32)
            block_rows = lax.dynamic_slice_in_dim(recent, block_id * UNK, UNK, 1)

            def take_band(lowest):
                return lax.dynamic_slice_in_dim(block_rows, (lowest - 1).astype(jnp.int32), BAND, 0)

            slices = jax.vmap(take_band)(delays[block_id]).astype(jnp.float32)
            product = jnp.einsum("cwij,cwjr->cir", matrices, slices, precision=lax.Precision.HIGHEST)
            live_slots = jnp.arange(SLOTS, dtype=jnp.int32) < counts[block_id]
            onehot = ((targets[block_id][None, :] == jnp.arange(11, dtype=jnp.int32)[:, None]) & live_slots[None, :]).astype(jnp.float32)
            return jnp.einsum("sc,cir->sir", onehot, product, precision=lax.Precision.HIGHEST)

        stencil = lax.map(block_terms, jnp.arange(BLOCKS, dtype=jnp.int32))
        stencil = stencil.reshape(N_GROUP, N_DEV, 11, UNK, EXC)
        padded = jnp.pad(stencil, ((1, 1), (2, 2), (0, 0), (0, 0), (0, 0)))
        field_sum = jnp.zeros((N_GROUP, N_DEV, UNK, EXC), jnp.float32)
        for target_code in range(11):
            grp_step, dev_step = code_offsets(target_code)
            field_sum = field_sum + padded[1 - grp_step:1 - grp_step + N_GROUP, 2 - dev_step:2 - dev_step + N_DEV, target_code]
        field_sum = field_sum.reshape(UNKNOWNS, EXC)
        right_side = (incident[moment].astype(jnp.float32) - field_sum).astype(jnp.bfloat16)
        blocks_rhs = right_side.reshape(BLOCKS, UNK, EXC).astype(jnp.float32)
        current = jnp.einsum("bij,bjr->bir", diag_inverse.astype(jnp.float32), blocks_rhs, precision=lax.Precision.HIGHEST)
        current = current.astype(jnp.bfloat16).reshape(UNKNOWNS, EXC)
        outputs.append(current)
        recent = jnp.concatenate([current[None], recent[:-1]], axis=0)
    return jnp.stack(outputs)
```

```python
import functools

import jax
import jax.numpy as jnp
from jax import lax
from jax.experimental import pallas as pl
from jax.experimental.pallas import tpu as pltpu
from jax.sharding import PartitionSpec as P

PAYLOADS = (("core", 0, 3), ("cross", 3, 2), ("cross_own", 5, 1), ("near", 6, 3), ("za", 9, 1), ("zb", 10, 1))


def swap_pairs(size, first, by=1):
    pairs = []
    for i in range(first, size - by, 2 * by):
        for j in range(i, min(i + by, size - by)):
            pairs += [(j, j + by), (j + by, j)]
    return pairs


def place_of(code, group_odd, dev_odd, pair_odd):
    near = code < 5
    up = code < 8
    off = jnp.where(near, code - 2, jnp.where(up, code - 6, code - 9))
    sub = jnp.where(off == 0, 2, jnp.where(off == 1 - 2 * dev_odd, 0, 1))
    to_core = up == (group_odd == 0)
    crossing = jnp.where(to_core, 0, 3) + sub
    far = jnp.where(off == 2 - 4 * pair_odd, 9, 10)
    close = jnp.where(jnp.abs(off) == 2, far, 6 + sub)
    return jnp.where(near, close, crossing)


def places(targets):
    slots = targets.shape[1]
    group = lax.axis_index("group")
    dev = lax.axis_index("dev")
    args = (lax.rem(group, 2), lax.rem(dev, 2), lax.rem(lax.div(dev, 2), 2))
    return [place_of(targets[0, c], *args) for c in range(slots)]


def in_hbm(array):
    return pltpu.with_memory_space_constraint(array, pltpu.HBM)


def fetch(sources, held, sems):
    copies = [pltpu.make_async_copy(source, ref, sems.at[i]) for i, (source, ref) in enumerate(zip(sources, held))]
    for copy in copies:
        copy.start()
    return copies


def slot_kernel(shift, parts, *refs):
    meta, (couplings, history), refs = refs[:3], refs[3:5], refs[5:]
    outs = refs[: len(parts)]
    targets, delays, counts, place, flags, weights, bands, total, zero, in_sems, out_sems, sems = refs[len(parts) :]
    copies = fetch(meta, (targets, delays, counts), sems)
    zero[...] = jnp.zeros_like(zero)
    for copy in copies:
        copy.wait()
    slots = targets.shape[1]
    band = couplings.shape[2]
    low = parts[0][1]
    high = parts[-1][1] + parts[-1][2]
    at = places(targets)
    live = [(c < counts[0]) & (at[c] >= low) & (at[c] < high) for c in range(slots)]

    def band_copies(c):
        lowest = delays[0, c] - 1 - shift
        if shift == 0:
            return [(None, pltpu.make_async_copy(history.at[pl.ds(lowest, band)], bands.at[c], in_sems.at[1, c]))]
        whole = pltpu.make_async_copy(
            history.at[pl.ds(jnp.maximum(lowest, 0), band)], bands.at[c], in_sems.at[1, c]
        )
        later = pltpu.make_async_copy(
            history.at[pl.ds(0, band - 1)], bands.at[c, pl.ds(1, band - 1)], in_sems.at[1, c]
        )
        return [(lowest >= 0, whole), (lowest < 0, later)]

    for c in range(slots):
        @pl.when(live[c])
        def _(c=c):
            pltpu.make_async_copy(couplings.at[0, c], weights.at[c], in_sems.at[0, c]).start()
            for cond, copy in band_copies(c):
                if cond is None:
                    copy.start()
                else:
                    pl.when(cond)(copy.start)
            if shift:
                @pl.when(delays[0, c] - 1 - shift < 0)
                def _():
                    bands[c, 0] = jnp.zeros(bands.shape[2:], bands.dtype)

    for c in range(slots):
        before = functools.reduce(jnp.logical_or, [live[b] & (at[b] == at[c]) for b in range(c)], False)
        after = functools.reduce(jnp.logical_or, [live[b] & (at[b] == at[c]) for b in range(c + 1, slots)], False)
        place[c] = at[c] - low
        flags[0, c] = live[c].astype(jnp.int32)
        flags[1, c] = jnp.int32(before) if isinstance(before, bool) else before.astype(jnp.int32)
        flags[2, c] = jnp.int32(after) if isinstance(after, bool) else after.astype(jnp.int32)

    row_copies = []
    for (_, first, rows), out in zip(parts, outs):
        for r in range(rows):
            p = first + r
            used = functools.reduce(jnp.logical_or, [live[c] & (at[c] == p) for c in range(slots)])
            row_copies.append((p - low, out.at[r], used))
    for p, out, used in row_copies:
        @pl.when(jnp.logical_not(used))
        def _(p=p, out=out):
            pltpu.make_async_copy(zero, out, out_sems.at[p]).start()

    def step(c, carry):
        @pl.when(flags[0, c] != 0)
        def _():
            pltpu.make_async_copy(couplings.at[0, c], weights.at[c], in_sems.at[0, c]).wait()
            if shift == 0:
                pltpu.make_async_copy(history.at[pl.ds(0, band)], bands.at[c], in_sems.at[1, c]).wait()
            else:
                @pl.when(delays[0, c] - 1 - shift >= 0)
                def _():
                    pltpu.make_async_copy(history.at[pl.ds(0, band)], bands.at[c], in_sems.at[1, c]).wait()

                @pl.when(delays[0, c] - 1 - shift < 0)
                def _():
                    pltpu.make_async_copy(
                        history.at[pl.ds(0, band - 1)], bands.at[c, pl.ds(1, band - 1)], in_sems.at[1, c]
                    ).wait()
            lhs = jnp.concatenate([weights[c, w] for w in range(band)], axis=1)
            rhs = bands[c].reshape(band * bands.shape[2], bands.shape[3])
            product = jnp.dot(lhs, rhs, preferred_element_type=jnp.float32)
            p = place[c]

            @pl.when(flags[1, c] == 0)
            def _():
                total[p] = product

            @pl.when(flags[1, c] != 0)
            def _():
                total[p] += product

            for q, out, _ in row_copies:
                @pl.when((p == q) & (flags[2, c] == 0))
                def _(q=q, out=out):
                    pltpu.make_async_copy(total.at[q], out, out_sems.at[q]).start()

        return carry

    lax.fori_loop(0, slots, step, 0)
    for p, out, _ in row_copies:
        pltpu.make_async_copy(zero, out, out_sems.at[p]).wait()


def slot_terms(shift, parts, couplings, history, targets, delays, counts):
    _, slots, band, unknowns, _ = couplings.shape
    width = history.shape[2]
    rows = sum(part[2] for part in parts)
    flops = 2 * slots * band * unknowns * unknowns * width // 2
    return pl.pallas_call(
        functools.partial(slot_kernel, shift, parts),
        out_shape=[jax.ShapeDtypeStruct((part[2], unknowns, width), jnp.float32) for part in parts],
        in_specs=[pl.BlockSpec(memory_space=pl.ANY)] * 5,
        out_specs=[pl.BlockSpec(memory_space=pl.ANY)] * len(parts),
        scratch_shapes=[
            pltpu.SMEM(targets.shape, jnp.int32),
            pltpu.SMEM(delays.shape, jnp.int32),
            pltpu.SMEM(counts.shape, jnp.int32),
            pltpu.SMEM((slots,), jnp.int32),
            pltpu.SMEM((3, slots), jnp.int32),
            pltpu.VMEM((slots, band, unknowns, unknowns), jnp.bfloat16),
            pltpu.VMEM((slots, band, unknowns, width), jnp.bfloat16),
            pltpu.VMEM((rows, unknowns, width), jnp.float32),
            pltpu.VMEM((unknowns, width), jnp.float32),
            pltpu.SemaphoreType.DMA((2, slots)),
            pltpu.SemaphoreType.DMA((rows,)),
            pltpu.SemaphoreType.DMA((3,)),
        ],
        compiler_params=pltpu.CompilerParams(vmem_limit_bytes=40 * 2**20),
        cost_estimate=pl.CostEstimate(flops=flops, bytes_accessed=10 * 2**20, transcendentals=0),
    )(targets, delays, counts, in_hbm(couplings), in_hbm(history))


def march_kernel(*refs):
    n = len(PAYLOADS)
    meta, (couplings, inverse, incident, partial, last_y, last_skew) = refs[:3], refs[3:9]
    outs = refs[9 + n : 9 + 2 * n]
    current = refs[9 + 2 * n]
    targets, delays, counts, weights, held, in_sems, sem, sems = refs[10 + 2 * n :]
    for copy in fetch(meta, (targets, delays, counts), sems):
        copy.wait()
    slots = targets.shape[1]
    at = places(targets)
    fresh = [(c < counts[0]) & (delays[0, c] == 1) for c in range(slots)]
    for c in range(slots):
        @pl.when(fresh[c])
        def _(c=c):
            pltpu.make_async_copy(couplings.at[0, c, 0], weights.at[c], in_sems.at[c]).start()
    field = partial[0] + last_y[0] + last_skew[0]
    right = (incident[0].astype(jnp.float32) - field).astype(jnp.bfloat16)
    current[...] = jnp.dot(inverse[0], right, preferred_element_type=jnp.float32).astype(jnp.bfloat16)
    for c in range(slots):
        @pl.when(fresh[c])
        def _(c=c):
            pltpu.make_async_copy(couplings.at[0, c, 0], weights.at[c], in_sems.at[c]).wait()
            for (_, first, rows), out in zip(PAYLOADS, outs):
                for r in range(rows):
                    @pl.when(at[c] == first + r)
                    def _(out=out, r=r):
                        copy = pltpu.make_async_copy(out.at[r], held, sem)
                        copy.start()
                        copy.wait()
            held[...] += jnp.dot(weights[c], current[...], preferred_element_type=jnp.float32)
            for (_, first, rows), out in zip(PAYLOADS, outs):
                for r in range(rows):
                    @pl.when(at[c] == first + r)
                    def _(out=out, r=r):
                        copy = pltpu.make_async_copy(held, out.at[r], sem)
                        copy.start()
                        copy.wait()


def march(couplings, inverse, incident, targets, delays, counts, sums, payloads):
    _, slots, _, unknowns, _ = couplings.shape
    width = incident.shape[2]
    n = len(payloads)
    vmem = pl.BlockSpec(memory_space=pltpu.VMEM)
    hbm = pl.BlockSpec(memory_space=pl.ANY)
    *updated, current = pl.pallas_call(
        march_kernel,
        out_shape=[jax.ShapeDtypeStruct(p.shape, p.dtype) for p in payloads]
        + [jax.ShapeDtypeStruct((unknowns, width), jnp.bfloat16)],
        in_specs=[pl.BlockSpec(memory_space=pl.ANY)] * 4 + [vmem] * 5 + [hbm] * n,
        out_specs=[hbm] * n + [vmem],
        input_output_aliases={9 + i: i for i in range(n)},
        scratch_shapes=[
            pltpu.SMEM(targets.shape, jnp.int32),
            pltpu.SMEM(delays.shape, jnp.int32),
            pltpu.SMEM(counts.shape, jnp.int32),
            pltpu.VMEM((slots, unknowns, unknowns), jnp.bfloat16),
            pltpu.VMEM((unknowns, width), jnp.float32),
            pltpu.SemaphoreType.DMA((slots,)),
            pltpu.SemaphoreType.DMA,
            pltpu.SemaphoreType.DMA((3,)),
        ],
        compiler_params=pltpu.CompilerParams(vmem_limit_bytes=24 * 2**20),
        cost_estimate=pl.CostEstimate(flops=2 * unknowns * unknowns * width, bytes_accessed=2**21, transcendentals=0),
    )(targets, delays, counts, in_hbm(couplings), inverse, incident, *sums, *payloads)
    return current, updated


def finish_kernel(inverse, incident, partial, last_y, last_skew, earlier, out):
    field = partial[0] + last_y[0] + last_skew[0]
    right = (incident[1].astype(jnp.float32) - field).astype(jnp.bfloat16)
    out[0] = earlier[...]
    out[1] = jnp.dot(inverse[0], right, preferred_element_type=jnp.float32).astype(jnp.bfloat16)


def finish(inverse, incident, sums, earlier):
    vmem = pl.BlockSpec(memory_space=pltpu.VMEM)
    return pl.pallas_call(
        finish_kernel,
        out_shape=jax.ShapeDtypeStruct(incident.shape, jnp.bfloat16),
        in_specs=[vmem] * 6,
        out_specs=vmem,
        compiler_params=pltpu.CompilerParams(vmem_limit_bytes=16 * 2**20),
    )(inverse, incident, *sums, earlier)


def deliver(groups, devs, payloads):
    core, cross, cross_own, near, za, zb = payloads
    inner = list(range(groups))
    outer = [0] + ([groups - 1] if groups % 2 == 0 and groups > 1 else [])
    inner = [g for g in inner if g not in outer]

    def within(value, members, pairs):
        listed = [(g * devs + a, g * devs + b) for g in members for a, b in pairs]
        return lax.ppermute(value, ("group", "dev"), listed)

    y_pairs, skew_pairs = swap_pairs(devs, 0), swap_pairs(devs, 1)
    cross_in = lax.ppermute(cross, "group", swap_pairs(groups, 1))
    core_in = lax.ppermute(core, "group", swap_pairs(groups, 0))
    joined = near + core_in
    outer_y = within(joined[0:1], outer, y_pairs)
    outer_skew = within(joined[1:2], outer, skew_pairs)
    za_in = lax.ppermute(za, "dev", swap_pairs(devs, 0, 2))
    zb_in = lax.ppermute(zb, "dev", swap_pairs(devs, 2, 2))
    inner_y = within(joined[0:1] + cross_in[0:1], inner, y_pairs)
    inner_skew = within(joined[1:2] + cross_in[1:2], inner, skew_pairs)
    own_in = lax.ppermute(cross_own, "group", swap_pairs(groups, 1))
    partial = joined[2:3] + own_in + za_in + zb_in + outer_y + outer_skew
    return partial, inner_y, inner_skew


def shards(groups, devs, couplings, history, inverse, incident, targets, delays, counts):
    meta = (targets, delays, counts)
    first = slot_terms(0, PAYLOADS[:2], couplings, history, *meta)
    second = slot_terms(0, PAYLOADS[2:], couplings, history, *meta)
    later = slot_terms(1, PAYLOADS, couplings, history, *meta)
    sums = deliver(groups, devs, (*first, *second))
    current, payloads = march(couplings, inverse, incident, *meta, sums, later)
    sums = deliver(groups, devs, payloads)
    return finish(inverse, incident, sums, current)


def solution(mesh):
    placed = (
        P(("group", "dev"), None, None, None, None),
        P(None, ("group", "dev"), None),
        P(("group", "dev"), None, None),
        P(None, ("group", "dev"), None),
        P(("group", "dev"), None),
        P(("group", "dev"), None),
        P(("group", "dev")),
    )
    return jax.shard_map(
        functools.partial(shards, mesh.shape["group"], mesh.shape["dev"]),
        mesh=mesh,
        in_specs=placed,
        out_specs=P(None, ("group", "dev"), None),
        check_vma=False,
    )
```

```python
import functools

import jax
import jax.numpy as jnp
from jax import lax
from jax.experimental import pallas as pl
from jax.experimental.pallas import tpu as pltpu
from jax.sharding import PartitionSpec as P

PAYLOADS = (("core", 0, 3), ("cross_y", 3, 1), ("cross_skew", 4, 1), ("cross_own", 5, 1), ("near", 6, 3), ("za", 9, 1), ("zb", 10, 1))


def swap_pairs(size, first, by=1):
    pairs = []
    for i in range(first, size - by, 2 * by):
        for j in range(i, min(i + by, size - by)):
            pairs += [(j, j + by), (j + by, j)]
    return pairs


def place_of(code, group_odd, dev_odd, pair_odd):
    near = code < 5
    up = code < 8
    off = jnp.where(near, code - 2, jnp.where(up, code - 6, code - 9))
    sub = jnp.where(off == 0, 2, jnp.where(off == 1 - 2 * dev_odd, 0, 1))
    to_core = up == (group_odd == 0)
    crossing = jnp.where(to_core, 0, 3) + sub
    far = jnp.where(off == 2 - 4 * pair_odd, 9, 10)
    close = jnp.where(jnp.abs(off) == 2, far, 6 + sub)
    return jnp.where(near, close, crossing)


def places(targets):
    slots = targets.shape[1]
    group = lax.axis_index("group")
    dev = lax.axis_index("dev")
    args = (lax.rem(group, 2), lax.rem(dev, 2), lax.rem(lax.div(dev, 2), 2))
    return [place_of(targets[0, c], *args) for c in range(slots)]


def in_hbm(array):
    return pltpu.with_memory_space_constraint(array, pltpu.HBM)


def fetch(sources, held, sems):
    copies = [pltpu.make_async_copy(source, ref, sems.at[i]) for i, (source, ref) in enumerate(zip(sources, held))]
    for copy in copies:
        copy.start()
    return copies


def slot_kernel(shift, parts, *refs):
    meta, (couplings, history), refs = refs[:3], refs[3:5], refs[5:]
    outs = refs[: len(parts)]
    targets, delays, counts, place, flags, weights, bands, total, zero, in_sems, out_sems, sems = refs[len(parts) :]
    copies = fetch(meta, (targets, delays, counts), sems)
    zero[...] = jnp.zeros_like(zero)
    for copy in copies:
        copy.wait()
    slots = targets.shape[1]
    band = couplings.shape[2]
    low = parts[0][1]
    high = parts[-1][1] + parts[-1][2]
    at = places(targets)
    live = [(c < counts[0]) & (at[c] >= low) & (at[c] < high) for c in range(slots)]

    def band_copies(c):
        lowest = delays[0, c] - 1 - shift
        if shift == 0:
            return [(None, pltpu.make_async_copy(history.at[pl.ds(lowest, band)], bands.at[c], in_sems.at[1, c]))]
        whole = pltpu.make_async_copy(
            history.at[pl.ds(jnp.maximum(lowest, 0), band)], bands.at[c], in_sems.at[1, c]
        )
        later = pltpu.make_async_copy(
            history.at[pl.ds(0, band - 1)], bands.at[c, pl.ds(1, band - 1)], in_sems.at[1, c]
        )
        return [(lowest >= 0, whole), (lowest < 0, later)]

    for c in range(slots):
        @pl.when(live[c])
        def _(c=c):
            pltpu.make_async_copy(couplings.at[0, c], weights.at[c], in_sems.at[0, c]).start()
            for cond, copy in band_copies(c):
                if cond is None:
                    copy.start()
                else:
                    pl.when(cond)(copy.start)
            if shift:
                @pl.when(delays[0, c] - 1 - shift < 0)
                def _():
                    bands[c, 0] = jnp.zeros(bands.shape[2:], bands.dtype)

    for c in range(slots):
        before = functools.reduce(jnp.logical_or, [live[b] & (at[b] == at[c]) for b in range(c)], False)
        after = functools.reduce(jnp.logical_or, [live[b] & (at[b] == at[c]) for b in range(c + 1, slots)], False)
        place[c] = at[c] - low
        flags[0, c] = live[c].astype(jnp.int32)
        flags[1, c] = jnp.int32(before) if isinstance(before, bool) else before.astype(jnp.int32)
        flags[2, c] = jnp.int32(after) if isinstance(after, bool) else after.astype(jnp.int32)

    row_copies = []
    for (_, first, rows), out in zip(parts, outs):
        for r in range(rows):
            p = first + r
            used = functools.reduce(jnp.logical_or, [live[c] & (at[c] == p) for c in range(slots)])
            row_copies.append((p - low, out.at[r], used))
    for p, out, used in row_copies:
        @pl.when(jnp.logical_not(used))
        def _(p=p, out=out):
            pltpu.make_async_copy(zero, out, out_sems.at[p]).start()

    def step(c, carry):
        @pl.when(flags[0, c] != 0)
        def _():
            pltpu.make_async_copy(couplings.at[0, c], weights.at[c], in_sems.at[0, c]).wait()
            if shift == 0:
                pltpu.make_async_copy(history.at[pl.ds(0, band)], bands.at[c], in_sems.at[1, c]).wait()
            else:
                @pl.when(delays[0, c] - 1 - shift >= 0)
                def _():
                    pltpu.make_async_copy(history.at[pl.ds(0, band)], bands.at[c], in_sems.at[1, c]).wait()

                @pl.when(delays[0, c] - 1 - shift < 0)
                def _():
                    pltpu.make_async_copy(
                        history.at[pl.ds(0, band - 1)], bands.at[c, pl.ds(1, band - 1)], in_sems.at[1, c]
                    ).wait()
            lhs = jnp.concatenate([weights[c, w] for w in range(band)], axis=1)
            rhs = bands[c].reshape(band * bands.shape[2], bands.shape[3])
            product = jnp.dot(lhs, rhs, preferred_element_type=jnp.float32)
            p = place[c]

            @pl.when(flags[1, c] == 0)
            def _():
                total[p] = product

            @pl.when(flags[1, c] != 0)
            def _():
                total[p] += product

            for q, out, _ in row_copies:
                @pl.when((p == q) & (flags[2, c] == 0))
                def _(q=q, out=out):
                    pltpu.make_async_copy(total.at[q], out, out_sems.at[q]).start()

        return carry

    lax.fori_loop(0, slots, step, 0)
    for p, out, _ in row_copies:
        pltpu.make_async_copy(zero, out, out_sems.at[p]).wait()


def slot_terms(shift, parts, couplings, history, targets, delays, counts):
    _, slots, band, unknowns, _ = couplings.shape
    width = history.shape[2]
    rows = sum(part[2] for part in parts)
    flops = 2 * slots * band * unknowns * unknowns * width // 2
    return pl.pallas_call(
        functools.partial(slot_kernel, shift, parts),
        out_shape=[jax.ShapeDtypeStruct((part[2], unknowns, width), jnp.float32) for part in parts],
        in_specs=[pl.BlockSpec(memory_space=pl.ANY)] * 5,
        out_specs=[pl.BlockSpec(memory_space=pl.ANY)] * len(parts),
        scratch_shapes=[
            pltpu.SMEM(targets.shape, jnp.int32),
            pltpu.SMEM(delays.shape, jnp.int32),
            pltpu.SMEM(counts.shape, jnp.int32),
            pltpu.SMEM((slots,), jnp.int32),
            pltpu.SMEM((3, slots), jnp.int32),
            pltpu.VMEM((slots, band, unknowns, unknowns), jnp.bfloat16),
            pltpu.VMEM((slots, band, unknowns, width), jnp.bfloat16),
            pltpu.VMEM((rows, unknowns, width), jnp.float32),
            pltpu.VMEM((unknowns, width), jnp.float32),
            pltpu.SemaphoreType.DMA((2, slots)),
            pltpu.SemaphoreType.DMA((rows,)),
            pltpu.SemaphoreType.DMA((3,)),
        ],
        compiler_params=pltpu.CompilerParams(vmem_limit_bytes=40 * 2**20),
        cost_estimate=pl.CostEstimate(flops=flops, bytes_accessed=10 * 2**20, transcendentals=0),
    )(in_hbm(targets), in_hbm(delays), counts, in_hbm(couplings), in_hbm(history))


def field_of(terms):
    near, core_in, *arrived = terms
    return functools.reduce(lambda a, b: a + b, [near[2], core_in[2]] + [term[0] for term in arrived])


def march_kernel(*refs):
    n = len(PAYLOADS)
    meta, (couplings, inverse, incident), terms = refs[:3], refs[3:6], refs[6:13]
    outs = refs[13 + n : 13 + 2 * n]
    current = refs[13 + 2 * n]
    targets, delays, counts, weights, held, in_sems, sem, sems = refs[14 + 2 * n :]
    for copy in fetch(meta, (targets, delays, counts), sems):
        copy.wait()
    slots = targets.shape[1]
    at = places(targets)
    fresh = [(c < counts[0]) & (delays[0, c] == 1) for c in range(slots)]
    for c in range(slots):
        @pl.when(fresh[c])
        def _(c=c):
            pltpu.make_async_copy(couplings.at[0, c, 0], weights.at[c], in_sems.at[c]).start()
    field = field_of(terms)
    right = (incident[0].astype(jnp.float32) - field).astype(jnp.bfloat16)
    current[...] = jnp.dot(inverse[0], right, preferred_element_type=jnp.float32).astype(jnp.bfloat16)
    for c in range(slots):
        @pl.when(fresh[c])
        def _(c=c):
            pltpu.make_async_copy(couplings.at[0, c, 0], weights.at[c], in_sems.at[c]).wait()
            for (_, first, rows), out in zip(PAYLOADS, outs):
                for r in range(rows):
                    @pl.when(at[c] == first + r)
                    def _(out=out, r=r):
                        copy = pltpu.make_async_copy(out.at[r], held, sem)
                        copy.start()
                        copy.wait()
            held[...] += jnp.dot(weights[c], current[...], preferred_element_type=jnp.float32)
            for (_, first, rows), out in zip(PAYLOADS, outs):
                for r in range(rows):
                    @pl.when(at[c] == first + r)
                    def _(out=out, r=r):
                        copy = pltpu.make_async_copy(held, out.at[r], sem)
                        copy.start()
                        copy.wait()


def march(couplings, inverse, incident, targets, delays, counts, sums, payloads):
    _, slots, _, unknowns, _ = couplings.shape
    width = incident.shape[2]
    n = len(payloads)
    vmem = pl.BlockSpec(memory_space=pltpu.VMEM)
    hbm = pl.BlockSpec(memory_space=pl.ANY)
    *updated, current = pl.pallas_call(
        march_kernel,
        out_shape=[jax.ShapeDtypeStruct(p.shape, p.dtype) for p in payloads]
        + [jax.ShapeDtypeStruct((unknowns, width), jnp.bfloat16)],
        in_specs=[pl.BlockSpec(memory_space=pl.ANY)] * 4 + [vmem] * 9 + [hbm] * n,
        out_specs=[hbm] * n + [vmem],
        input_output_aliases={13 + i: i for i in range(n)},
        scratch_shapes=[
            pltpu.SMEM(targets.shape, jnp.int32),
            pltpu.SMEM(delays.shape, jnp.int32),
            pltpu.SMEM(counts.shape, jnp.int32),
            pltpu.VMEM((slots, unknowns, unknowns), jnp.bfloat16),
            pltpu.VMEM((unknowns, width), jnp.float32),
            pltpu.SemaphoreType.DMA((slots,)),
            pltpu.SemaphoreType.DMA,
            pltpu.SemaphoreType.DMA((3,)),
        ],
        compiler_params=pltpu.CompilerParams(vmem_limit_bytes=24 * 2**20),
        cost_estimate=pl.CostEstimate(flops=2 * unknowns * unknowns * width, bytes_accessed=2**21, transcendentals=0),
    )(in_hbm(targets), in_hbm(delays), counts, in_hbm(couplings), inverse, incident, *sums, *payloads)
    return current, updated


def finish_kernel(inverse, incident, *refs):
    *terms, earlier, out = refs
    field = field_of(terms)
    right = (incident[1].astype(jnp.float32) - field).astype(jnp.bfloat16)
    out[0] = earlier[...]
    out[1] = jnp.dot(inverse[0], right, preferred_element_type=jnp.float32).astype(jnp.bfloat16)


def finish(inverse, incident, sums, earlier):
    vmem = pl.BlockSpec(memory_space=pltpu.VMEM)
    return pl.pallas_call(
        finish_kernel,
        out_shape=jax.ShapeDtypeStruct(incident.shape, jnp.bfloat16),
        in_specs=[vmem] * (3 + len(sums)),
        out_specs=vmem,
        compiler_params=pltpu.CompilerParams(vmem_limit_bytes=16 * 2**20),
    )(inverse, incident, *sums, earlier)


def on_chip(kernel, *operands, carried=()):
    vmem = pl.BlockSpec(memory_space=pltpu.VMEM)
    hbm = pl.BlockSpec(memory_space=pl.ANY)
    return pl.pallas_call(
        kernel,
        out_shape=[jax.ShapeDtypeStruct(operands[0].shape, jnp.float32)]
        + [jax.ShapeDtypeStruct(c.shape, c.dtype) for c in carried],
        in_specs=[vmem] * len(operands) + [hbm] * len(carried),
        out_specs=[vmem] + [hbm] * len(carried),
        input_output_aliases={len(operands) + i: 1 + i for i in range(len(carried))},
        compiler_params=pltpu.CompilerParams(vmem_limit_bytes=16 * 2**20),
    )(*operands, *carried)


def join_kernel(row, arrived, near, core_in, *refs):
    total = refs[len(refs) // 2]
    total[0] = arrived[0] + near[row] + core_in[row]


def deliver(groups, devs, payloads):
    core, cross_y, cross_skew, cross_own, near, za, zb = payloads
    x_pairs = swap_pairs(groups, 1)
    skew_in = lax.ppermute(cross_skew, "group", x_pairs)
    y_in = lax.ppermute(cross_y, "group", x_pairs)
    core_in = lax.ppermute(core, "group", swap_pairs(groups, 0))
    za_in = lax.ppermute(za, "dev", swap_pairs(devs, 0, 2))
    zb_in = lax.ppermute(zb, "dev", swap_pairs(devs, 2, 2))
    (skew,) = on_chip(functools.partial(join_kernel, 1), skew_in, near, core_in)
    skew_in = lax.ppermute(skew, "dev", swap_pairs(devs, 1))
    y, cross_own = on_chip(functools.partial(join_kernel, 0), y_in, near, core_in, carried=(cross_own,))
    y_in = lax.ppermute(y, "dev", swap_pairs(devs, 0))
    own_in = lax.ppermute(cross_own, "group", x_pairs)
    return near, core_in, za_in, zb_in, own_in, skew_in, y_in


def shards(groups, devs, couplings, history, inverse, incident, targets, delays, counts):
    meta = (targets, delays, counts)
    first = slot_terms(0, PAYLOADS[:3], couplings, history, *meta)
    second = slot_terms(0, PAYLOADS[3:], couplings, history, *meta)
    later = slot_terms(1, PAYLOADS, couplings, history, *meta)
    sums = deliver(groups, devs, (*first, *second))
    current, payloads = march(couplings, inverse, incident, *meta, sums, later)
    sums = deliver(groups, devs, payloads)
    return finish(inverse, incident, sums, current)


def solution(mesh):
    placed = (
        P(("group", "dev"), None, None, None, None),
        P(None, ("group", "dev"), None),
        P(("group", "dev"), None, None),
        P(None, ("group", "dev"), None),
        P(("group", "dev"), None),
        P(("group", "dev"), None),
        P(("group", "dev")),
    )
    return jax.shard_map(
        functools.partial(shards, mesh.shape["group"], mesh.shape["dev"]),
        mesh=mesh,
        in_specs=placed,
        out_specs=P(None, ("group", "dev"), None),
        check_vma=False,
    )
```

```python
import functools

import jax
import jax.numpy as jnp
from jax import lax
from jax.experimental import pallas as pl
from jax.experimental.pallas import tpu as pltpu
from jax.sharding import PartitionSpec as P

CORE, NEAR, CROSS, ZA, ZB = 0, 3, 6, 9, 10
PAYLOADS = (
    ("core", CORE, 3),
    ("near", NEAR, 3),
    ("cross_y", CROSS, 1),
    ("cross_skew", CROSS + 1, 1),
    ("cross_own", CROSS + 2, 1),
    ("za", ZA, 1),
    ("zb", ZB, 1),
)


def swap_pairs(size, first, by=1):
    pairs = []
    for i in range(first, size - by, 2 * by):
        for j in range(i, min(i + by, size - by)):
            pairs += [(j, j + by), (j + by, j)]
    return pairs


def far_pairs(groups, devs, turn):
    return [
        (g * devs + a, g * devs + b)
        for g in range(groups)
        for a, b in swap_pairs(devs, 2 * ((g + turn) % 2), 2)
    ]


def places(targets):
    group, dev = lax.axis_index("group"), lax.axis_index("dev")
    group_odd, dev_odd, pair_odd = lax.rem(group, 2), lax.rem(dev, 2), lax.rem(lax.div(dev, 2), 2)
    at, useful = [], []
    for c in range(targets.shape[1]):
        code = targets[0, c]
        near = code < 5
        up = code < 8
        off = jnp.where(near, code - 2, jnp.where(up, code - 6, code - 9))
        sub = jnp.where(off == 0, 2, jnp.where(off == 1 - 2 * dev_odd, 0, 1))
        to_core = up == (group_odd == 0)
        crossing = jnp.where(to_core, CORE + sub, CROSS + sub)
        far = jnp.where(off == 2 - 4 * lax.rem(pair_odd + group_odd, 2), ZA, ZB)
        close = jnp.where(jnp.abs(off) == 2, far, NEAR + sub)
        at.append(jnp.where(near, close, crossing))
        to_group = group + jnp.where(near, 0, jnp.where(up, 1, -1))
        to_dev = dev + off
        inside = (to_group >= 0) & (to_group < lax.axis_size("group"))
        useful.append(inside & (to_dev >= 0) & (to_dev < lax.axis_size("dev")))
    return at, useful


def in_hbm(array):
    return pltpu.with_memory_space_constraint(array, pltpu.HBM)


def fetch(sources, held, sems):
    copies = [pltpu.make_async_copy(source, ref, sems.at[i]) for i, (source, ref) in enumerate(zip(sources, held))]
    for copy in copies:
        copy.start()
    return copies


def rows_of(parts, outs):
    return [(first + r, out, r) for (_, first, rows), out in zip(parts, outs) for r in range(rows)]


def slot_kernel(shift, parts, unread, *refs):
    meta, (couplings, history), refs = refs[:3], refs[3:5], refs[5 + unread :]
    outs = refs[: len(parts)]
    targets, delays, counts, place, flags, weights, bands, total, in_sems, sems = refs[len(parts) :]
    for copy in fetch(meta, (targets, delays, counts), sems):
        copy.wait()
    slots = targets.shape[1]
    band = couplings.shape[2]
    rows = rows_of(parts, outs)
    at, useful = places(targets)
    live = []
    for c in range(slots):
        wanted = (at[c] >= rows[0][0]) & (at[c] <= rows[-1][0])
        live.append((c < counts[0]) & useful[c] & wanted)

    def copies_of(c, early):
        matrices = pltpu.make_async_copy(couplings.at[0, c], weights.at[c], in_sems.at[0, c])
        if early:
            source = history.at[pl.ds(0, band - 1)]
            steps = pltpu.make_async_copy(source, bands.at[c, pl.ds(1, band - 1)], in_sems.at[1, c])
        else:
            source = history.at[pl.ds(jnp.maximum(delays[0, c] - 1 - shift, 0), band)]
            steps = pltpu.make_async_copy(source, bands.at[c], in_sems.at[1, c])
        return matrices, steps

    def each(c, act):
        if shift == 0:
            act(copies_of(c, False))
            return
        early = delays[0, c] <= shift

        @pl.when(early)
        def _():
            act(copies_of(c, True))

        @pl.when(jnp.logical_not(early))
        def _():
            act(copies_of(c, False))

    def start(copies):
        for copy in copies:
            copy.start()

    def wait(copies):
        for copy in copies:
            copy.wait()

    for c in range(slots):
        @pl.when(live[c])
        def _(c=c):
            each(c, start)
            if shift:
                @pl.when(delays[0, c] <= shift)
                def _():
                    bands[c, 0] = jnp.zeros(bands.shape[2:], bands.dtype)

    for c in range(slots):
        place[c] = at[c]
        flags[0, c] = live[c].astype(jnp.int32)
        repeats = [(live[b] & (at[b] == at[c])).astype(jnp.int32) for b in range(c)]
        flags[1, c] = functools.reduce(lambda x, y: x | y, repeats, jnp.int32(0))

    for p, out, r in rows:
        used = functools.reduce(jnp.logical_or, [live[c] & (at[c] == p) for c in range(slots)])

        @pl.when(jnp.logical_not(used))
        def _(out=out, r=r):
            out[r] = jnp.zeros(out.shape[1:], out.dtype)

    def step(c, carry):
        @pl.when(flags[0, c] != 0)
        def _():
            each(c, wait)
            lhs = jnp.concatenate([weights[c, w] for w in range(band)], axis=1)
            rhs = bands[c].reshape(band * bands.shape[2], bands.shape[3])
            total[...] = jnp.dot(lhs, rhs, preferred_element_type=jnp.float32)
            for p, out, r in rows:
                @pl.when((place[c] == p) & (flags[1, c] == 0))
                def _(out=out, r=r):
                    out[r] = total[...]

                @pl.when((place[c] == p) & (flags[1, c] != 0))
                def _(out=out, r=r):
                    out[r] += total[...]

        return carry

    lax.fori_loop(0, slots, step, 0)


def slot_terms(shift, parts, couplings, history, targets, delays, counts, earlier=()):
    _, slots, band, unknowns, _ = couplings.shape
    width = history.shape[2]
    flops = slots * band * unknowns * unknowns * width
    return pl.pallas_call(
        functools.partial(slot_kernel, shift, parts, len(earlier)),
        out_shape=[jax.ShapeDtypeStruct((part[2], unknowns, width), jnp.float32) for part in parts],
        in_specs=[pl.BlockSpec(memory_space=pl.ANY)] * (5 + len(earlier)),
        out_specs=[pl.BlockSpec(memory_space=pltpu.VMEM)] * len(parts),
        scratch_shapes=[
            pltpu.SMEM(targets.shape, jnp.int32),
            pltpu.SMEM(delays.shape, jnp.int32),
            pltpu.SMEM(counts.shape, jnp.int32),
            pltpu.SMEM((slots,), jnp.int32),
            pltpu.SMEM((2, slots), jnp.int32),
            pltpu.VMEM((slots, band, unknowns, unknowns), jnp.bfloat16),
            pltpu.VMEM((slots, band, unknowns, width), jnp.bfloat16),
            pltpu.VMEM((unknowns, width), jnp.float32),
            pltpu.SemaphoreType.DMA((2, slots)),
            pltpu.SemaphoreType.DMA((3,)),
        ],
        compiler_params=pltpu.CompilerParams(vmem_limit_bytes=30 * 2**20),
        cost_estimate=pl.CostEstimate(flops=flops, bytes_accessed=10 * 2**20, transcendentals=0),
    )(in_hbm(targets), in_hbm(delays), counts, in_hbm(couplings), in_hbm(history), *earlier)


def march_kernel(*refs):
    n = len(PAYLOADS)
    meta, (couplings, inverse, incident), terms = refs[:3], refs[3:6], refs[6:8]
    outs = refs[8 + n : 8 + 2 * n]
    current = refs[8 + 2 * n]
    targets, delays, counts, weights, held, in_sems, sem, sems = refs[9 + 2 * n :]
    for copy in fetch(meta, (targets, delays, counts), sems):
        copy.wait()
    slots = targets.shape[1]
    at, useful = places(targets)
    fresh = [(c < counts[0]) & (delays[0, c] == 1) & useful[c] for c in range(slots)]
    for c in range(slots):
        @pl.when(fresh[c])
        def _(c=c):
            pltpu.make_async_copy(couplings.at[0, c, 0], weights.at[c], in_sems.at[c]).start()
    field = terms[0][0] + terms[1][0]
    right = (incident[0].astype(jnp.float32) - field).astype(jnp.bfloat16)
    current[...] = jnp.dot(inverse[0], right, preferred_element_type=jnp.float32).astype(jnp.bfloat16)
    for c in range(slots):
        @pl.when(fresh[c])
        def _(c=c):
            pltpu.make_async_copy(couplings.at[0, c, 0], weights.at[c], in_sems.at[c]).wait()
            for p, out, r in rows_of(PAYLOADS, outs):
                @pl.when(at[c] == p)
                def _(out=out, r=r):
                    copy = pltpu.make_async_copy(out.at[r], held, sem)
                    copy.start()
                    copy.wait()
            held[...] += jnp.dot(weights[c], current[...], preferred_element_type=jnp.float32)
            for p, out, r in rows_of(PAYLOADS, outs):
                @pl.when(at[c] == p)
                def _(out=out, r=r):
                    copy = pltpu.make_async_copy(held, out.at[r], sem)
                    copy.start()
                    copy.wait()


def march(couplings, inverse, incident, targets, delays, counts, sums, payloads):
    _, slots, _, unknowns, _ = couplings.shape
    width = incident.shape[2]
    n = len(payloads)
    vmem = pl.BlockSpec(memory_space=pltpu.VMEM)
    hbm = pl.BlockSpec(memory_space=pl.ANY)
    *updated, current = pl.pallas_call(
        march_kernel,
        out_shape=[jax.ShapeDtypeStruct(p.shape, p.dtype) for p in payloads]
        + [jax.ShapeDtypeStruct((unknowns, width), jnp.bfloat16)],
        in_specs=[pl.BlockSpec(memory_space=pl.ANY)] * 4 + [vmem] * 4 + [hbm] * n,
        out_specs=[hbm] * n + [vmem],
        input_output_aliases={8 + i: i for i in range(n)},
        scratch_shapes=[
            pltpu.SMEM(targets.shape, jnp.int32),
            pltpu.SMEM(delays.shape, jnp.int32),
            pltpu.SMEM(counts.shape, jnp.int32),
            pltpu.VMEM((slots, unknowns, unknowns), jnp.bfloat16),
            pltpu.VMEM((unknowns, width), jnp.float32),
            pltpu.SemaphoreType.DMA((slots,)),
            pltpu.SemaphoreType.DMA,
            pltpu.SemaphoreType.DMA((3,)),
        ],
        compiler_params=pltpu.CompilerParams(vmem_limit_bytes=24 * 2**20),
        cost_estimate=pl.CostEstimate(flops=2 * unknowns * unknowns * width, bytes_accessed=2**21, transcendentals=0),
    )(in_hbm(targets), in_hbm(delays), counts, in_hbm(couplings), inverse, incident, *sums, *payloads)
    return current, updated


def finish_kernel(inverse, incident, *refs):
    *terms, earlier, out = refs
    field = terms[0][0] + terms[1][0]
    right = (incident[1].astype(jnp.float32) - field).astype(jnp.bfloat16)
    out[0] = earlier[...]
    out[1] = jnp.dot(inverse[0], right, preferred_element_type=jnp.float32).astype(jnp.bfloat16)


def finish(inverse, incident, sums, earlier):
    vmem = pl.BlockSpec(memory_space=pltpu.VMEM)
    return pl.pallas_call(
        finish_kernel,
        out_shape=jax.ShapeDtypeStruct(incident.shape, jnp.bfloat16),
        in_specs=[vmem] * (3 + len(sums)),
        out_specs=vmem,
        compiler_params=pltpu.CompilerParams(vmem_limit_bytes=16 * 2**20),
    )(inverse, incident, *sums, earlier)


def stage(kernel, operands, carried=()):
    vmem = pl.BlockSpec(memory_space=pltpu.VMEM)
    hbm = pl.BlockSpec(memory_space=pl.ANY)
    sums = [jax.ShapeDtypeStruct(operands[0].shape, jnp.float32)]
    return pl.pallas_call(
        kernel,
        out_shape=sums + [jax.ShapeDtypeStruct(c.shape, c.dtype) for c in carried],
        in_specs=[vmem] * len(operands) + [hbm] * len(carried),
        out_specs=[vmem] * len(sums) + [hbm] * len(carried),
        input_output_aliases={len(operands) + i: len(sums) + i for i in range(len(carried))},
        compiler_params=pltpu.CompilerParams(vmem_limit_bytes=16 * 2**20),
    )(*operands, *carried)


def join_kernel(row, arrived, near, core_in, *refs):
    total = refs[len(refs) // 2]
    total[0] = arrived[0] + near[row] + core_in[row]


def sum_kernel(*refs):
    *terms, total = refs
    total[...] = functools.reduce(lambda a, b: a + b, [term[...] for term in terms])


def deliver(groups, devs, payloads):
    core, near, cross_y, cross_skew, cross_own, za, zb = payloads
    x_pairs = swap_pairs(groups, 1)
    y_in = lax.ppermute(cross_y, "group", x_pairs)
    skew_in = lax.ppermute(cross_skew, "group", x_pairs)
    core_in = lax.ppermute(core, "group", swap_pairs(groups, 0))
    za_in = lax.ppermute(za, ("group", "dev"), far_pairs(groups, devs, 0))
    y, zb = stage(functools.partial(join_kernel, 0), (y_in, near, core_in), (zb,))
    y_in = lax.ppermute(y, "dev", swap_pairs(devs, 0))
    zb_in = lax.ppermute(zb, ("group", "dev"), far_pairs(groups, devs, 1))
    skew, own = stage(functools.partial(join_kernel, 1), (skew_in, near, core_in), (cross_own,))
    skew_in = lax.ppermute(skew, "dev", swap_pairs(devs, 1))
    own_in = lax.ppermute(own, "group", x_pairs)
    (field,) = stage(functools.partial(join_kernel, 2), (za_in, near, core_in))
    (field,) = stage(sum_kernel, (field, y_in))
    (field,) = stage(sum_kernel, (field, zb_in))
    (field,) = stage(sum_kernel, (field, skew_in))
    return field, own_in


def shards(groups, devs, couplings, history, inverse, incident, targets, delays, counts):
    meta = (targets, delays, counts)
    first = slot_terms(0, PAYLOADS[:4], couplings, history, *meta)
    second = slot_terms(0, PAYLOADS[4:], couplings, history, *meta, first[:1])
    later = slot_terms(1, PAYLOADS, couplings, history, *meta)
    sums = deliver(groups, devs, (*first, *second))
    current, payloads = march(couplings, inverse, incident, *meta, sums, later)
    sums = deliver(groups, devs, payloads)
    return finish(inverse, incident, sums, current)


def solution(mesh):
    placed = (
        P(("group", "dev"), None, None, None, None),
        P(None, ("group", "dev"), None),
        P(("group", "dev"), None, None),
        P(None, ("group", "dev"), None),
        P(("group", "dev"), None),
        P(("group", "dev"), None),
        P(("group", "dev")),
    )
    return jax.shard_map(
        functools.partial(shards, mesh.shape["group"], mesh.shape["dev"]),
        mesh=mesh,
        in_specs=placed,
        out_specs=P(None, ("group", "dev"), None),
        check_vma=False,
    )
```

```python
import functools

import jax
import jax.numpy as jnp
from jax import lax
from jax.experimental import pallas as pl
from jax.experimental.pallas import tpu as pltpu
from jax.sharding import PartitionSpec as P

CORE, NEAR, CROSS, ZA, ZB = 0, 3, 6, 9, 10
PAYLOADS = (
    ("core", CORE, 3),
    ("near", NEAR, 3),
    ("cross_y", CROSS, 1),
    ("cross_skew", CROSS + 1, 1),
    ("cross_own", CROSS + 2, 1),
    ("za", ZA, 1),
    ("zb", ZB, 1),
)


def swap_pairs(size, first, by=1):
    pairs = []
    for i in range(first, size - by, 2 * by):
        for j in range(i, min(i + by, size - by)):
            pairs += [(j, j + by), (j + by, j)]
    return pairs


def far_pairs(groups, devs, turn):
    return [
        (g * devs + a, g * devs + b)
        for g in range(groups)
        for a, b in swap_pairs(devs, 2 - 2 * turn, 2)
    ]


def places(targets):
    group, dev = lax.axis_index("group"), lax.axis_index("dev")
    group_odd, dev_odd, pair_odd = lax.rem(group, 2), lax.rem(dev, 2), lax.rem(lax.div(dev, 2), 2)
    at, useful = [], []
    for c in range(targets.shape[1]):
        code = targets[0, c]
        near = code < 5
        up = code < 8
        off = jnp.where(near, code - 2, jnp.where(up, code - 6, code - 9))
        sub = jnp.where(off == 0, 2, jnp.where(off == 1 - 2 * dev_odd, 0, 1))
        to_core = up == (group_odd == 0)
        crossing = jnp.where(to_core, CORE + sub, CROSS + sub)
        far = jnp.where(off == 2 - 4 * pair_odd, ZB, ZA)
        close = jnp.where(jnp.abs(off) == 2, far, NEAR + sub)
        at.append(jnp.where(near, close, crossing))
        to_group = group + jnp.where(near, 0, jnp.where(up, 1, -1))
        to_dev = dev + off
        inside = (to_group >= 0) & (to_group < lax.axis_size("group"))
        useful.append(inside & (to_dev >= 0) & (to_dev < lax.axis_size("dev")))
    return at, useful


def in_hbm(array):
    return pltpu.with_memory_space_constraint(array, pltpu.HBM)


def fetch(sources, held, sems):
    copies = [pltpu.make_async_copy(source, ref, sems.at[i]) for i, (source, ref) in enumerate(zip(sources, held))]
    for copy in copies:
        copy.start()
    return copies


def rows_of(parts, outs):
    return [(first + r, out, r) for (_, first, rows), out in zip(parts, outs) for r in range(rows)]


def slot_kernel(shift, parts, unread, *refs):
    meta, (couplings, history), refs = refs[:3], refs[3:5], refs[5 + unread :]
    outs = refs[: len(parts)]
    targets, delays, counts, place, weights, bands, total, in_sems, sems = refs[len(parts) :]
    copies = fetch(meta, (targets, delays, counts), sems)
    rows = rows_of(parts, outs)
    for _, out, r in rows:
        out[r] = jnp.zeros(out.shape[1:], out.dtype)
    for copy in copies:
        copy.wait()
    slots = targets.shape[1]
    band = couplings.shape[2]
    at, useful = places(targets)
    live = []
    for c in range(slots):
        wanted = (at[c] >= rows[0][0]) & (at[c] <= rows[-1][0])
        live.append((c < counts[0]) & useful[c] & wanted)

    def copies_of(c, early):
        matrices = pltpu.make_async_copy(couplings.at[0, c], weights.at[c], in_sems.at[0, c])
        if early:
            source = history.at[pl.ds(0, band - 1)]
            steps = pltpu.make_async_copy(source, bands.at[c, pl.ds(1, band - 1)], in_sems.at[1, c])
        else:
            source = history.at[pl.ds(jnp.maximum(delays[0, c] - 1 - shift, 0), band)]
            steps = pltpu.make_async_copy(source, bands.at[c], in_sems.at[1, c])
        return matrices, steps

    def each(c, act):
        if shift == 0:
            act(copies_of(c, False))
            return
        early = delays[0, c] <= shift

        @pl.when(early)
        def _():
            act(copies_of(c, True))

        @pl.when(jnp.logical_not(early))
        def _():
            act(copies_of(c, False))

    def start(copies):
        for copy in copies:
            copy.start()

    def wait(copies):
        for copy in copies:
            copy.wait()

    for c in range(slots):
        @pl.when(live[c])
        def _(c=c):
            each(c, start)
            if shift:
                @pl.when(delays[0, c] <= shift)
                def _():
                    bands[c, 0] = jnp.zeros(bands.shape[2:], bands.dtype)

    for c in range(slots):
        place[c] = jnp.where(live[c], at[c], -1)

    def step(c, carry):
        @pl.when(place[c] >= 0)
        def _():
            each(c, wait)
            lhs = jnp.concatenate([weights[c, w] for w in range(band)], axis=1)
            rhs = bands[c].reshape(band * bands.shape[2], bands.shape[3])
            total[...] = jnp.dot(lhs, rhs, preferred_element_type=jnp.float32)
            for p, out, r in rows:
                @pl.when(place[c] == p)
                def _(out=out, r=r):
                    out[r] += total[...]

        return carry

    lax.fori_loop(0, slots, step, 0)


def slot_terms(shift, parts, couplings, history, targets, delays, counts, earlier=()):
    _, slots, band, unknowns, _ = couplings.shape
    width = history.shape[2]
    flops = slots * band * unknowns * unknowns * width
    return pl.pallas_call(
        functools.partial(slot_kernel, shift, parts, len(earlier)),
        out_shape=[jax.ShapeDtypeStruct((part[2], unknowns, width), jnp.float32) for part in parts],
        in_specs=[pl.BlockSpec(memory_space=pl.ANY)] * (5 + len(earlier)),
        out_specs=[pl.BlockSpec(memory_space=pltpu.VMEM)] * len(parts),
        scratch_shapes=[
            pltpu.SMEM(targets.shape, jnp.int32),
            pltpu.SMEM(delays.shape, jnp.int32),
            pltpu.SMEM(counts.shape, jnp.int32),
            pltpu.SMEM((slots,), jnp.int32),
            pltpu.VMEM((slots, band, unknowns, unknowns), jnp.bfloat16),
            pltpu.VMEM((slots, band, unknowns, width), jnp.bfloat16),
            pltpu.VMEM((unknowns, width), jnp.float32),
            pltpu.SemaphoreType.DMA((2, slots)),
            pltpu.SemaphoreType.DMA((3,)),
        ],
        compiler_params=pltpu.CompilerParams(vmem_limit_bytes=30 * 2**20),
        cost_estimate=pl.CostEstimate(flops=flops, bytes_accessed=10 * 2**20, transcendentals=0),
    )(in_hbm(targets), in_hbm(delays), counts, in_hbm(couplings), in_hbm(history), *earlier)


def march_kernel(*refs):
    n = len(PAYLOADS)
    meta, (couplings, inverse, incident), terms = refs[:3], refs[3:6], refs[6:8]
    outs = refs[8 + n : 8 + 2 * n]
    current = refs[8 + 2 * n]
    targets, delays, counts, weights, held, in_sems, sem, sems = refs[9 + 2 * n :]
    for copy in fetch(meta, (targets, delays, counts), sems):
        copy.wait()
    slots = targets.shape[1]
    at, useful = places(targets)
    fresh = [(c < counts[0]) & (delays[0, c] == 1) & useful[c] for c in range(slots)]
    for c in range(slots):
        @pl.when(fresh[c])
        def _(c=c):
            pltpu.make_async_copy(couplings.at[0, c, 0], weights.at[c], in_sems.at[c]).start()
    field = terms[0][0] + terms[1][0]
    right = (incident[0].astype(jnp.float32) - field).astype(jnp.bfloat16)
    current[...] = jnp.dot(inverse[0], right, preferred_element_type=jnp.float32).astype(jnp.bfloat16)
    for c in range(slots):
        @pl.when(fresh[c])
        def _(c=c):
            pltpu.make_async_copy(couplings.at[0, c, 0], weights.at[c], in_sems.at[c]).wait()
            for p, out, r in rows_of(PAYLOADS, outs):
                @pl.when(at[c] == p)
                def _(out=out, r=r):
                    copy = pltpu.make_async_copy(out.at[r], held, sem)
                    copy.start()
                    copy.wait()
            held[...] += jnp.dot(weights[c], current[...], preferred_element_type=jnp.float32)
            for p, out, r in rows_of(PAYLOADS, outs):
                @pl.when(at[c] == p)
                def _(out=out, r=r):
                    copy = pltpu.make_async_copy(held, out.at[r], sem)
                    copy.start()
                    copy.wait()


def march(couplings, inverse, incident, targets, delays, counts, sums, payloads):
    _, slots, _, unknowns, _ = couplings.shape
    width = incident.shape[2]
    n = len(payloads)
    vmem = pl.BlockSpec(memory_space=pltpu.VMEM)
    hbm = pl.BlockSpec(memory_space=pl.ANY)
    *updated, current = pl.pallas_call(
        march_kernel,
        out_shape=[jax.ShapeDtypeStruct(p.shape, p.dtype) for p in payloads]
        + [jax.ShapeDtypeStruct((unknowns, width), jnp.bfloat16)],
        in_specs=[pl.BlockSpec(memory_space=pl.ANY)] * 4 + [vmem] * 4 + [hbm] * n,
        out_specs=[hbm] * n + [vmem],
        input_output_aliases={8 + i: i for i in range(n)},
        scratch_shapes=[
            pltpu.SMEM(targets.shape, jnp.int32),
            pltpu.SMEM(delays.shape, jnp.int32),
            pltpu.SMEM(counts.shape, jnp.int32),
            pltpu.VMEM((slots, unknowns, unknowns), jnp.bfloat16),
            pltpu.VMEM((unknowns, width), jnp.float32),
            pltpu.SemaphoreType.DMA((slots,)),
            pltpu.SemaphoreType.DMA,
            pltpu.SemaphoreType.DMA((3,)),
        ],
        compiler_params=pltpu.CompilerParams(vmem_limit_bytes=24 * 2**20),
        cost_estimate=pl.CostEstimate(flops=2 * unknowns * unknowns * width, bytes_accessed=2**21, transcendentals=0),
    )(in_hbm(targets), in_hbm(delays), counts, in_hbm(couplings), inverse, incident, *sums, *payloads)
    return current, updated


def finish_kernel(inverse, incident, *refs):
    *terms, earlier, out = refs
    field = terms[0][0] + terms[1][0]
    right = (incident[1].astype(jnp.float32) - field).astype(jnp.bfloat16)
    out[0] = earlier[...]
    out[1] = jnp.dot(inverse[0], right, preferred_element_type=jnp.float32).astype(jnp.bfloat16)


def finish(inverse, incident, sums, earlier):
    vmem = pl.BlockSpec(memory_space=pltpu.VMEM)
    return pl.pallas_call(
        finish_kernel,
        out_shape=jax.ShapeDtypeStruct(incident.shape, jnp.bfloat16),
        in_specs=[vmem] * (3 + len(sums)),
        out_specs=vmem,
        compiler_params=pltpu.CompilerParams(vmem_limit_bytes=16 * 2**20),
    )(inverse, incident, *sums, earlier)


def stage(kernel, operands, carried=()):
    vmem = pl.BlockSpec(memory_space=pltpu.VMEM)
    hbm = pl.BlockSpec(memory_space=pl.ANY)
    sums = [jax.ShapeDtypeStruct(operands[0].shape, jnp.float32)]
    return pl.pallas_call(
        kernel,
        out_shape=sums + [jax.ShapeDtypeStruct(c.shape, c.dtype) for c in carried],
        in_specs=[vmem] * len(operands) + [hbm] * len(carried),
        out_specs=[vmem] * len(sums) + [hbm] * len(carried),
        input_output_aliases={len(operands) + i: len(sums) + i for i in range(len(carried))},
        compiler_params=pltpu.CompilerParams(vmem_limit_bytes=16 * 2**20),
    )(*operands, *carried)


def join_kernel(row, arrived, near, core_in, *refs):
    total = refs[len(refs) // 2]
    total[0] = arrived[0] + near[row] + core_in[row]


def sum_kernel(*refs):
    *terms, total = refs
    total[...] = functools.reduce(lambda a, b: a + b, [term[...] for term in terms])


def deliver(groups, devs, payloads):
    core, near, cross_y, cross_skew, cross_own, za, zb = payloads
    x_pairs = swap_pairs(groups, 1)
    y_in = lax.ppermute(cross_y, "group", x_pairs)
    skew_in = lax.ppermute(cross_skew, "group", x_pairs)
    core_in = lax.ppermute(core, "group", swap_pairs(groups, 0))
    za_in = lax.ppermute(za, ("group", "dev"), far_pairs(groups, devs, 0))
    y, zb = stage(functools.partial(join_kernel, 0), (y_in, near, core_in), (zb,))
    y_in = lax.ppermute(y, "dev", swap_pairs(devs, 0))
    zb_in = lax.ppermute(zb, ("group", "dev"), far_pairs(groups, devs, 1))
    skew, cross_own = stage(functools.partial(join_kernel, 1), (skew_in, near, core_in), (cross_own,))
    skew_in = lax.ppermute(skew, "dev", swap_pairs(devs, 1))
    own_in = lax.ppermute(cross_own, "group", x_pairs)
    (field,) = stage(functools.partial(join_kernel, 2), (za_in, near, core_in))
    (field,) = stage(sum_kernel, (field, y_in))
    (field,) = stage(sum_kernel, (field, zb_in))
    (field,) = stage(sum_kernel, (field, skew_in))
    return field, own_in


def shards(groups, devs, couplings, history, inverse, incident, targets, delays, counts):
    meta = (targets, delays, counts)
    first = slot_terms(0, PAYLOADS[:4], couplings, history, *meta)
    second = slot_terms(0, PAYLOADS[4:], couplings, history, *meta, first[:1])
    later = slot_terms(1, PAYLOADS, couplings, history, *meta)
    sums = deliver(groups, devs, (*first, *second))
    current, payloads = march(couplings, inverse, incident, *meta, sums, later)
    sums = deliver(groups, devs, payloads)
    return finish(inverse, incident, sums, current)


def solution(mesh):
    placed = (
        P(("group", "dev"), None, None, None, None),
        P(None, ("group", "dev"), None),
        P(("group", "dev"), None, None),
        P(None, ("group", "dev"), None),
        P(("group", "dev"), None),
        P(("group", "dev"), None),
        P(("group", "dev")),
    )
    return jax.shard_map(
        functools.partial(shards, mesh.shape["group"], mesh.shape["dev"]),
        mesh=mesh,
        in_specs=placed,
        out_specs=P(None, ("group", "dev"), None),
        check_vma=False,
    )
```

```python
import functools

import jax
import jax.numpy as jnp
from jax import lax
from jax.experimental import pallas as pl
from jax.experimental.pallas import tpu as pltpu
from jax.sharding import PartitionSpec as P

CORE, NEAR, CROSS, ZA, ZB = 0, 3, 6, 9, 10
PAYLOADS = (
    ("core", CORE, 3),
    ("near", NEAR, 3),
    ("cross_y", CROSS, 1),
    ("cross_skew", CROSS + 1, 1),
    ("cross_own", CROSS + 2, 1),
    ("za", ZA, 1),
    ("zb", ZB, 1),
)


def swap_pairs(size, first, by=1):
    pairs = []
    for i in range(first, size - by, 2 * by):
        for j in range(i, min(i + by, size - by)):
            pairs += [(j, j + by), (j + by, j)]
    return pairs


def far_pairs(groups, devs, turn):
    return [
        (g * devs + a, g * devs + b)
        for g in range(groups)
        for a, b in swap_pairs(devs, 2 - 2 * turn, 2)
    ]


def places(targets):
    group, dev = lax.axis_index("group"), lax.axis_index("dev")
    group_odd, dev_odd, pair_odd = lax.rem(group, 2), lax.rem(dev, 2), lax.rem(lax.div(dev, 2), 2)
    at, useful = [], []
    for c in range(targets.shape[1]):
        code = targets[0, c]
        near = code < 5
        up = code < 8
        off = jnp.where(near, code - 2, jnp.where(up, code - 6, code - 9))
        sub = jnp.where(off == 0, 2, jnp.where(off == 1 - 2 * dev_odd, 0, 1))
        to_core = up == (group_odd == 0)
        crossing = jnp.where(to_core, CORE + sub, CROSS + sub)
        far = jnp.where(off == 2 - 4 * pair_odd, ZB, ZA)
        close = jnp.where(jnp.abs(off) == 2, far, NEAR + sub)
        at.append(jnp.where(near, close, crossing))
        to_group = group + jnp.where(near, 0, jnp.where(up, 1, -1))
        to_dev = dev + off
        inside = (to_group >= 0) & (to_group < lax.axis_size("group"))
        useful.append(inside & (to_dev >= 0) & (to_dev < lax.axis_size("dev")))
    return at, useful


def in_hbm(array):
    return pltpu.with_memory_space_constraint(array, pltpu.HBM)


def fetch(sources, held, sems):
    copies = [pltpu.make_async_copy(source, ref, sems.at[i]) for i, (source, ref) in enumerate(zip(sources, held))]
    for copy in copies:
        copy.start()
    return copies


def rows_of(parts, outs):
    return [(first + r, out, r) for (_, first, rows), out in zip(parts, outs) for r in range(rows)]


def slot_kernel(shift, parts, unread, *refs):
    meta, (couplings, history), refs = refs[:3], refs[3:5], refs[5 + unread :]
    outs = refs[: len(parts)]
    targets, delays, counts, place, weights, bands, total, in_sems, sems = refs[len(parts) :]
    copies = fetch(meta, (targets, delays, counts), sems)
    rows = rows_of(parts, outs)
    for _, out, r in rows:
        out[r] = jnp.zeros(out.shape[1:], out.dtype)
    for copy in copies:
        copy.wait()
    slots = targets.shape[1]
    band = couplings.shape[2]
    at, useful = places(targets)
    live = []
    for c in range(slots):
        wanted = (at[c] >= rows[0][0]) & (at[c] <= rows[-1][0])
        live.append((c < counts[0]) & useful[c] & wanted)

    def copies_of(c, early):
        matrices = pltpu.make_async_copy(couplings.at[0, c], weights.at[c], in_sems.at[0, c])
        if early:
            source = history.at[pl.ds(0, band - 1)]
            steps = pltpu.make_async_copy(source, bands.at[c, pl.ds(1, band - 1)], in_sems.at[1, c])
        else:
            source = history.at[pl.ds(jnp.maximum(delays[0, c] - 1 - shift, 0), band)]
            steps = pltpu.make_async_copy(source, bands.at[c], in_sems.at[1, c])
        return matrices, steps

    def each(c, act):
        if shift == 0:
            act(copies_of(c, False))
            return
        early = delays[0, c] <= shift

        @pl.when(early)
        def _():
            act(copies_of(c, True))

        @pl.when(jnp.logical_not(early))
        def _():
            act(copies_of(c, False))

    def start(copies):
        for copy in copies:
            copy.start()

    def wait(copies):
        for copy in copies:
            copy.wait()

    for c in range(slots):
        @pl.when(live[c])
        def _(c=c):
            each(c, start)
            if shift:
                @pl.when(delays[0, c] <= shift)
                def _():
                    bands[c, 0] = jnp.zeros(bands.shape[2:], bands.dtype)

    for c in range(slots):
        place[c] = jnp.where(live[c], at[c], -1)

    def step(c, carry):
        @pl.when(place[c] >= 0)
        def _():
            each(c, wait)
            lhs = jnp.concatenate([weights[c, w] for w in range(band)], axis=1)
            rhs = bands[c].reshape(band * bands.shape[2], bands.shape[3])
            total[...] = jnp.dot(lhs, rhs, preferred_element_type=jnp.float32)
            for p, out, r in rows:
                @pl.when(place[c] == p)
                def _(out=out, r=r):
                    out[r] += total[...]

        return carry

    lax.fori_loop(0, slots, step, 0)


def slot_terms(shift, parts, couplings, history, targets, delays, counts, earlier=()):
    _, slots, band, unknowns, _ = couplings.shape
    width = history.shape[2]
    flops = slots * band * unknowns * unknowns * width
    return pl.pallas_call(
        functools.partial(slot_kernel, shift, parts, len(earlier)),
        out_shape=[jax.ShapeDtypeStruct((part[2], unknowns, width), jnp.float32) for part in parts],
        in_specs=[pl.BlockSpec(memory_space=pl.ANY)] * (5 + len(earlier)),
        out_specs=[pl.BlockSpec(memory_space=pltpu.VMEM)] * len(parts),
        scratch_shapes=[
            pltpu.SMEM(targets.shape, jnp.int32),
            pltpu.SMEM(delays.shape, jnp.int32),
            pltpu.SMEM(counts.shape, jnp.int32),
            pltpu.SMEM((slots,), jnp.int32),
            pltpu.VMEM((slots, band, unknowns, unknowns), jnp.bfloat16),
            pltpu.VMEM((slots, band, unknowns, width), jnp.bfloat16),
            pltpu.VMEM((unknowns, width), jnp.float32),
            pltpu.SemaphoreType.DMA((2, slots)),
            pltpu.SemaphoreType.DMA((3,)),
        ],
        compiler_params=pltpu.CompilerParams(vmem_limit_bytes=30 * 2**20),
        cost_estimate=pl.CostEstimate(flops=flops, bytes_accessed=10 * 2**20, transcendentals=0),
    )(in_hbm(targets), in_hbm(delays), counts, in_hbm(couplings), in_hbm(history), *earlier)


def march_kernel(*refs):
    n = len(PAYLOADS)
    meta, (couplings, inverse_hbm, incident_hbm), terms = refs[:3], refs[3:6], refs[6:8]
    outs = refs[8 + n : 8 + 2 * n]
    current = refs[8 + 2 * n]
    targets, delays, counts, inverse, incident, weights, held, in_sems, sem, sems = refs[9 + 2 * n :]
    sources = (*meta, incident_hbm.at[0], inverse_hbm.at[0])
    copies = fetch(sources, (targets, delays, counts, incident, inverse), sems)
    field = terms[0][0] + terms[1][0]
    copies[3].wait()
    right = (incident[...].astype(jnp.float32) - field).astype(jnp.bfloat16)
    for copy in copies[:3]:
        copy.wait()
    slots = targets.shape[1]
    at, useful = places(targets)
    fresh = [(c < counts[0]) & (delays[0, c] == 1) & useful[c] for c in range(slots)]
    for c in range(slots):
        @pl.when(fresh[c])
        def _(c=c):
            pltpu.make_async_copy(couplings.at[0, c, 0], weights.at[c], in_sems.at[c]).start()
    copies[4].wait()
    current[...] = jnp.dot(inverse[...], right, preferred_element_type=jnp.float32).astype(jnp.bfloat16)
    for c in range(slots):
        @pl.when(fresh[c])
        def _(c=c):
            pltpu.make_async_copy(couplings.at[0, c, 0], weights.at[c], in_sems.at[c]).wait()
            for p, out, r in rows_of(PAYLOADS, outs):
                @pl.when(at[c] == p)
                def _(out=out, r=r):
                    copy = pltpu.make_async_copy(out.at[r], held, sem)
                    copy.start()
                    copy.wait()
            held[...] += jnp.dot(weights[c], current[...], preferred_element_type=jnp.float32)
            for p, out, r in rows_of(PAYLOADS, outs):
                @pl.when(at[c] == p)
                def _(out=out, r=r):
                    copy = pltpu.make_async_copy(held, out.at[r], sem)
                    copy.start()
                    copy.wait()


def march(couplings, inverse, incident, targets, delays, counts, sums, payloads):
    _, slots, _, unknowns, _ = couplings.shape
    width = incident.shape[2]
    n = len(payloads)
    vmem = pl.BlockSpec(memory_space=pltpu.VMEM)
    hbm = pl.BlockSpec(memory_space=pl.ANY)
    *updated, current = pl.pallas_call(
        march_kernel,
        out_shape=[jax.ShapeDtypeStruct(p.shape, p.dtype) for p in payloads]
        + [jax.ShapeDtypeStruct((unknowns, width), jnp.bfloat16)],
        in_specs=[pl.BlockSpec(memory_space=pl.ANY)] * 6 + [vmem] * 2 + [hbm] * n,
        out_specs=[hbm] * n + [vmem],
        input_output_aliases={8 + i: i for i in range(n)},
        scratch_shapes=[
            pltpu.SMEM(targets.shape, jnp.int32),
            pltpu.SMEM(delays.shape, jnp.int32),
            pltpu.SMEM(counts.shape, jnp.int32),
            pltpu.VMEM((unknowns, unknowns), jnp.bfloat16),
            pltpu.VMEM((unknowns, width), jnp.bfloat16),
            pltpu.VMEM((slots, unknowns, unknowns), jnp.bfloat16),
            pltpu.VMEM((unknowns, width), jnp.float32),
            pltpu.SemaphoreType.DMA((slots,)),
            pltpu.SemaphoreType.DMA,
            pltpu.SemaphoreType.DMA((5,)),
        ],
        compiler_params=pltpu.CompilerParams(vmem_limit_bytes=24 * 2**20),
        cost_estimate=pl.CostEstimate(flops=2 * unknowns * unknowns * width, bytes_accessed=2**21, transcendentals=0),
    )(in_hbm(targets), in_hbm(delays), counts, in_hbm(couplings), in_hbm(inverse), in_hbm(incident), *sums, *payloads)
    return current, updated


def finish_kernel(inverse, incident, *refs):
    *terms, earlier, out = refs
    field = terms[0][0] + terms[1][0]
    right = (incident[1].astype(jnp.float32) - field).astype(jnp.bfloat16)
    out[0] = earlier[...]
    out[1] = jnp.dot(inverse[0], right, preferred_element_type=jnp.float32).astype(jnp.bfloat16)


def finish(inverse, incident, sums, earlier):
    vmem = pl.BlockSpec(memory_space=pltpu.VMEM)
    return pl.pallas_call(
        finish_kernel,
        out_shape=jax.ShapeDtypeStruct(incident.shape, jnp.bfloat16),
        in_specs=[vmem] * (3 + len(sums)),
        out_specs=vmem,
        compiler_params=pltpu.CompilerParams(vmem_limit_bytes=16 * 2**20),
    )(inverse, incident, *sums, earlier)


def stage(kernel, operands, carried=()):
    vmem = pl.BlockSpec(memory_space=pltpu.VMEM)
    hbm = pl.BlockSpec(memory_space=pl.ANY)
    sums = [jax.ShapeDtypeStruct(operands[0].shape, jnp.float32)]
    return pl.pallas_call(
        kernel,
        out_shape=sums + [jax.ShapeDtypeStruct(c.shape, c.dtype) for c in carried],
        in_specs=[vmem] * len(operands) + [hbm] * len(carried),
        out_specs=[vmem] * len(sums) + [hbm] * len(carried),
        input_output_aliases={len(operands) + i: len(sums) + i for i in range(len(carried))},
        compiler_params=pltpu.CompilerParams(vmem_limit_bytes=16 * 2**20),
    )(*operands, *carried)


def join_kernel(row, arrived, core_in, near, *refs):
    total = refs[len(refs) // 2]
    total[0] = arrived[0] + near[row] + core_in[row]


def sum_kernel(*refs):
    *terms, total = refs
    total[...] = functools.reduce(lambda a, b: a + b, [term[...] for term in terms])


def deliver(groups, devs, payloads):
    core, near, cross_y, cross_skew, cross_own, za, zb = payloads
    x_pairs = swap_pairs(groups, 1)
    y_in = lax.ppermute(cross_y, "group", x_pairs)
    skew_in = lax.ppermute(cross_skew, "group", x_pairs)
    core_in = lax.ppermute(core, "group", swap_pairs(groups, 0))
    za_in = lax.ppermute(za, ("group", "dev"), far_pairs(groups, devs, 0))
    y, zb = stage(functools.partial(join_kernel, 0), (y_in, core_in, near), (zb,))
    y_in = lax.ppermute(y, "dev", swap_pairs(devs, 0))
    zb_in = lax.ppermute(zb, ("group", "dev"), far_pairs(groups, devs, 1))
    skew, cross_own = stage(functools.partial(join_kernel, 1), (skew_in, core_in, near), (cross_own,))
    skew_in = lax.ppermute(skew, "dev", swap_pairs(devs, 1))
    own_in = lax.ppermute(cross_own, "group", x_pairs)
    (field,) = stage(functools.partial(join_kernel, 2), (za_in, core_in, near))
    (field,) = stage(sum_kernel, (field, y_in))
    (field,) = stage(sum_kernel, (field, zb_in))
    (field,) = stage(sum_kernel, (field, skew_in))
    return field, own_in


def shards(groups, devs, couplings, history, inverse, incident, targets, delays, counts):
    meta = (targets, delays, counts)
    first = slot_terms(0, PAYLOADS[:4], couplings, history, *meta)
    second = slot_terms(0, PAYLOADS[4:], couplings, history, *meta, first[:1])
    later = slot_terms(1, PAYLOADS, couplings, history, *meta)
    sums = deliver(groups, devs, (*first, *second))
    current, payloads = march(couplings, inverse, incident, *meta, sums, later)
    sums = deliver(groups, devs, payloads)
    return finish(inverse, incident, sums, current)


def solution(mesh):
    placed = (
        P(("group", "dev"), None, None, None, None),
        P(None, ("group", "dev"), None),
        P(("group", "dev"), None, None),
        P(None, ("group", "dev"), None),
        P(("group", "dev"), None),
        P(("group", "dev"), None),
        P(("group", "dev")),
    )
    return jax.shard_map(
        functools.partial(shards, mesh.shape["group"], mesh.shape["dev"]),
        mesh=mesh,
        in_specs=placed,
        out_specs=P(None, ("group", "dev"), None),
        check_vma=False,
    )
```
